256 devices in a mesh: col: 64 (over z, y, core), ga: 4 (over x).
Axes of the slice: x: 4, y: 4, z: 8, core: 2. Of those that a mesh axis runs over, the one named last changes fastest.
Arguments:
- cell_state: float32 [3, 90, 262144], P(None, None, ('col', 'ga')), may hold values from 0.01 to 1
- cell_parent: int32 [262144], P(('col', 'ga')), may hold values from 0 to 65535, as said below
- sunlit: int32 [65536], P(('col', 'ga')), may hold values from 0 to 1, as said below
- cos_zenith: float32 [65536], P(('col', 'ga')), may hold values from 0.1 to 1
- albedo: float32 [65536], P(('col', 'ga')), may hold values from 0.05 to 0.8
- gas_optics: float32 [4, 112], P(None, 'ga'), may hold values from 0.001 to 0.3
- solar_weight: float32 [112], P('ga'), may hold values from 0.002 to 0.02
Outputs:
- heating: float32 [90, 262144], P(None, ('col', 'ga'))
- surface_net: float32 [262144], P(('col', 'ga'))
The draws below stay inside these ranges and needn't reach their ends.
Inputs may be any that keep to these rules, and one draw needn't show every extreme that they name: `cell_parent`: the four cells of every parent column p lie in the aligned block of 1024 cells with index p // 256; every parent column has exactly four cells. Exactly 32768 parent columns are sunlit, and in every draw all 256 parent columns of some aligned block of 256 are sunlit.
All inputs are finite; a program needn't handle non-finite values.
Results may differ from the reference program's by a relative error of at most 0.0003.
Values sent between devices are 32-bit elements; how exact they have to be, the bound alone decides.
A program may use at most 128 MiB of HBM per device.

```python
import math
import jax
import jax.numpy as jnp
from jax import lax

LEV = 90
G = 112
PDYN = 256
PARENTS = 65536
CELLS = 262144


def draw_cell_parent(key, part):
    key = jax.random.fold_in(key, 11)
    blocks = PARENTS // PDYN
    key_list = jax.random.split(key, blocks)

    def one_block(block_key):
        return jax.random.permutation(block_key, 4 * PDYN) // 4
    local_parent = jax.vmap(one_block)(key_list)
    offsets = (jnp.arange(blocks, dtype=jnp.int32) * PDYN)[:, None]
    return (local_parent + offsets).reshape(-1).astype(jnp.int32)


def draw_sunlit(key, part):
    key = jax.random.fold_in(key, 23)
    first_key, second_key = jax.random.split(key)
    blocks = PARENTS // PDYN
    block_rank = jax.random.permutation(first_key, blocks).astype(jnp.int32)
    jitter = jax.random.randint(second_key, (PARENTS,), 0, 2 * PDYN, dtype=jnp.int32)
    scores = jnp.repeat(block_rank, PDYN) * PDYN + jitter
    ordering = jnp.argsort(scores, stable=True)
    ranking = jnp.argsort(ordering, stable=True)
    return (ranking < PARENTS // 2).astype(jnp.int32)


def level_of(rng, shape, cuts, smallest, high):
    loudness = 1.0
    for position, blocks in cuts:
        steps = jax.random.uniform(jax.random.fold_in(jax.random.fold_in(rng, 6), position), (blocks,), jnp.float32, smallest / len(cuts), high / len(cuts))
        loudness = loudness * jnp.repeat(jnp.exp(steps), shape[position] // blocks).reshape((-1,) + (1,) * (len(shape) - 1 - position))
    return loudness


def setup_inputs(seed: int = 0) -> dict:
    seeds = jax.random.split(jax.random.key(seed), 8)
    return {
        "cell_state": jnp.clip(jnp.exp(math.log(1.0) - 4.6051702 * jax.random.uniform(seeds[0], (3, LEV, CELLS), jnp.float32) ** level_of(seeds[0], (3, LEV, CELLS), ((2, 256),), -0.2, 0.2)), 0.01, 1.0),
        "cell_parent": draw_cell_parent(jax.random.fold_in(seeds[7], 71), 0),
        "sunlit": draw_sunlit(jax.random.fold_in(seeds[7], 71), 0),
        "cos_zenith": jnp.clip(0.1 + 0.9 * jax.random.uniform(seeds[3], (PARENTS,), jnp.float32) ** level_of(seeds[3], (PARENTS,), ((0, 256),), -0.2, 0.2), 0.1, 1.0),
        "albedo": jnp.clip(0.05 + 0.75 * jax.random.uniform(seeds[4], (PARENTS,), jnp.float32) ** level_of(seeds[4], (PARENTS,), ((0, 256),), -0.2, 0.2), 0.05, 0.8),
        "gas_optics": jnp.clip(jnp.exp(math.log(0.3) - 5.7037825 * jax.random.uniform(seeds[5], (4, G), jnp.float32) ** level_of(seeds[5], (4, G), ((1, 4),), -0.2, 0.2)), 0.001, 0.3),
        "solar_weight": jnp.clip(jnp.exp(math.log(0.02) - 2.30258502 * jax.random.uniform(seeds[6], (G,), jnp.float32) ** level_of(seeds[6], (G,), ((0, 4),), -0.2, 0.2)), 0.002, 0.02),
    }


def layer_optics(factors, vapour, ozone, cloud, cosine):
    tau = factors[0] * vapour + factors[1] * ozone + factors[2] + factors[3] * cloud
    cloud_scat = 0.9 * factors[3] * cloud
    scatter = factors[2] + cloud_scat
    omega = 0.95 * scatter / tau
    backward = 0.5 * (1.0 - 0.85 * cloud_scat / scatter)
    beam_pass = jnp.exp(-tau / cosine)
    spread = 2.0 * backward * omega * tau
    absorbed = jnp.exp(-1.66 * (1.0 - omega) * tau)
    reflect = absorbed * spread / (1.0 + spread)
    transmit = absorbed / (1.0 + spread)
    direct_up = omega * (1.0 - beam_pass) * backward
    direct_down = omega * (1.0 - beam_pass) * (1.0 - backward)
    return reflect, transmit, direct_up, direct_down, beam_pass


def radiate(records, gas_optics, solar_weight):
    levels = (records.shape[0] - 2) // 3
    vapour = records[:levels]
    ozone = records[levels:2 * levels]
    cloud = records[2 * levels:3 * levels]
    cosine = records[3 * levels]
    ground = records[3 * levels + 1]
    factors = gas_optics[:, :, None]
    weights = solar_weight[:, None]
    shape = (gas_optics.shape[1], records.shape[1])

    def upward(state_pair, inputs):
        albedo_dir, albedo_dif = state_pair
        reflect, transmit, direct_up, direct_down, beam_pass = layer_optics(factors, inputs[0], inputs[1], inputs[2], cosine)
        inverse = 1.0 / (1.0 - albedo_dif * reflect)
        new_dif = reflect + transmit * transmit * albedo_dif * inverse
        new_dir = direct_up + (beam_pass * albedo_dir + direct_down * albedo_dif) * transmit * inverse
        return (new_dir, new_dif), (albedo_dir, albedo_dif)

    initial = jnp.broadcast_to(ground[None, :], shape)
    (top_dir, top_dif), (below_dir, below_dif) = lax.scan(upward, (initial, initial), (vapour[::-1], ozone[::-1], cloud[::-1]))
    below_dir = below_dir[::-1]
    below_dif = below_dif[::-1]
    beam_top = jnp.broadcast_to(cosine[None, :], shape)
    top_net = jnp.sum(weights * (beam_top - top_dir * beam_top), axis=0)

    def downward(state_pair, inputs):
        beam, diffuse = state_pair
        reflect, transmit, direct_up, direct_down, beam_pass = layer_optics(factors, inputs[0], inputs[1], inputs[2], cosine)
        albedo_dir = inputs[3]
        albedo_dif = inputs[4]
        diffuse_next = (transmit * diffuse + reflect * beam_pass * beam * albedo_dir + direct_down * beam) / (1.0 - albedo_dif * reflect)
        beam_next = beam * beam_pass
        upwell = albedo_dir * beam_next + albedo_dif * diffuse_next
        net_flux = jnp.sum(weights * (beam_next + diffuse_next - upwell), axis=0)
        return (beam_next, diffuse_next), net_flux

    zeros_init = jnp.zeros(shape, jnp.float32)
    unused, nets = lax.scan(downward, (beam_top, zeros_init), (vapour, ozone, cloud, below_dir, below_dif))
    return jnp.concatenate([top_net[None, :], nets], axis=0)


def reference(cell_state, cell_parent, sunlit, cos_zenith, albedo, gas_optics, solar_weight):
    levels = cell_state.shape[1]
    flattened = cell_state.reshape(3 * levels, cell_state.shape[2]).T
    summed = jax.ops.segment_sum(flattened, cell_parent, num_segments=PARENTS)
    parent_state = summed.T * 0.25
    records = jnp.concatenate([parent_state, cos_zenith[None, :], albedo[None, :]], axis=0)

    def add_gpoint(running, inputs):
        return running + radiate(records, inputs[0][:, None], inputs[1][None]), None

    initial = jnp.zeros((levels + 1, PARENTS), jnp.float32)
    net_flux, unused = lax.scan(add_gpoint, initial, (gas_optics.T, solar_weight))
    net_flux = net_flux * sunlit.astype(jnp.float32)[None, :]
    heating = levels * (net_flux[:-1] - net_flux[1:])
    result_rows = jnp.concatenate([heating, net_flux[-1:]], axis=0)
    cell_rows = jnp.take(result_rows, cell_parent, axis=1)
    return cell_rows[:-1], cell_rows[-1]
```

```python
import functools

import jax
import jax.numpy as jnp
from jax import lax
from jax.experimental import pallas as pl
from jax.experimental.pallas import tpu as pltpu
from jax.sharding import PartitionSpec as P

MESH = pl.DeviceIdType.MESH
LOG2E = 1.4426950408889634
LANES = 128
ROWS = 8
BLOCKS = 2
UNROLL = 3
NT = (((1,), (1,)), ((), ()))
TN = (((0,), (0,)), ((), ()))


def split_dot(left, right, dims):
    high = left.astype(jnp.bfloat16)
    low = (left - high.astype(jnp.float32)).astype(jnp.bfloat16)
    first = lax.dot_general(high, right, dims, preferred_element_type=jnp.float32)
    return first + lax.dot_general(low, right, dims, preferred_element_type=jnp.float32)


def right_split_dot(left, right, dims):
    high = right.astype(jnp.bfloat16)
    low = (right - high.astype(jnp.float32)).astype(jnp.bfloat16)
    first = lax.dot_general(left, high, dims, preferred_element_type=jnp.float32)
    return first + lax.dot_general(left, low, dims, preferred_element_type=jnp.float32)


def inverse_of(value):
    return pl.reciprocal(value, approx=True)


def kernel(
    groups,
    state_hbm,
    parent_ref,
    sunlit_ref,
    cosine_ref,
    albedo_ref,
    gas_ref,
    weight_ref,
    heat_ref,
    surface_ref,
    state,
    member,
    wide,
    coef,
    mine,
    theirs,
    keep,
    total,
    column,
    local_sem,
    send_sem,
    recv_sem,
):
    fields, levels, cells = state.shape
    parents = member.shape[0]
    halves = parents // LANES
    local_g = gas_ref.shape[1]
    me = lax.axis_index("ga")

    loads = [
        pltpu.make_async_copy(state_hbm.at[f], state.at[f], local_sem.at[f])
        for f in range(fields)
    ]
    for load in loads:
        load.start()
    barrier = pltpu.get_barrier_semaphore()
    for d in range(1, groups):
        pl.semaphore_signal(
            barrier, inc=1, device_id={"ga": lax.rem(me + d, groups)}, device_id_type=MESH
        )

    mine[...] = jnp.zeros_like(mine)
    mine[0:4, 0:local_g] = gas_ref[...]
    mine[4:5, 0:local_g] = weight_ref[...]
    local_parent = parent_ref[...] % parents
    ids = lax.broadcasted_iota(jnp.int32, (parents, cells), 0)
    member[...] = jnp.where(ids == local_parent, 1.0, 0.0).astype(jnp.bfloat16)
    total[...] = jnp.zeros_like(total)
    column[0] = jnp.broadcast_to(cosine_ref[...], (ROWS, parents))
    column[1] = jnp.broadcast_to((-0.5 * LOG2E) / cosine_ref[...], (ROWS, parents))
    column[2] = jnp.broadcast_to(albedo_ref[...], (ROWS, parents))

    for f in range(fields):
        loads[f].wait()
        parent_state = split_dot(state[f], member[...], NT) * 0.25
        for l in range(levels):
            wide[f, l] = jnp.broadcast_to(parent_state[l : l + 1], (ROWS, parents))

    pl.semaphore_wait(barrier, groups - 1)
    sends = []
    for d in range(1, groups):
        send = pltpu.make_async_remote_copy(
            src_ref=mine,
            dst_ref=theirs.at[d - 1],
            send_sem=send_sem.at[d - 1],
            recv_sem=recv_sem.at[d - 1],
            device_id={"ga": lax.rem(me + d, groups)},
            device_id_type=MESH,
        )
        send.start()
        sends.append(send)

    spread_row = lax.broadcasted_iota(jnp.int32, (ROWS, 5 * LANES), 0)
    spread_lane = lax.broadcasted_iota(jnp.int32, (ROWS, 5 * LANES), 1) // LANES
    spread = jnp.where(spread_row == spread_lane, 1.0, 0.0)

    def set_coef(packed, row):
        flat = lax.dot_general(
            packed, spread, TN, precision=lax.Precision.HIGHEST,
            preferred_element_type=jnp.float32,
        )[:local_g]
        vapour, ozone, rayleigh, cloud, weight = [
            flat[:, k * LANES : (k + 1) * LANES] for k in range(5)
        ]
        rows = pl.ds(row, local_g)
        coef[0, rows, :] = 2.0 * vapour
        coef[1, rows, :] = 2.0 * ozone
        coef[2, rows, :] = (0.95 * 0.15 * 0.9) * cloud
        coef[3, rows, :] = 0.95 * rayleigh
        coef[4, rows, :] = 0.1 * rayleigh
        coef[5, rows, :] = weight

    pairs = [(i, h) for i in range(BLOCKS) for h in range(halves)]

    def lanes(h):
        return slice(h * LANES, (h + 1) * LANES)

    def chunk(index, carry):
        base = index * (BLOCKS * ROWS)
        factor = [
            [coef[k, pl.ds(pl.multiple_of(base + i * ROWS, ROWS), ROWS), :] for k in range(6)]
            for i in range(BLOCKS)
        ]

        def down(step, flux):
            flux = list(flux)
            for s in range(UNROLL):
                l = step * UNROLL + s
                sums = [None] * halves
                for n, (i, h) in enumerate(pairs):
                    above, diffuse, beam = flux[n]
                    net = beam + diffuse
                    sums[h] = net if sums[h] is None else sums[h] + net
                    vapour, ozone, cloud = [wide[f, l, :, lanes(h)] for f in range(fields)]
                    k0, k1, k3, scat, rest, unused = factor[i]
                    x = k3 * cloud
                    b = x + scat
                    e = x * (1.58175 / 0.12825) + scat
                    absorb = (k0 * vapour + k1 * ozone) + (x * (0.29 / 0.12825) + rest)
                    tau = absorb + (b + e)
                    passed = beam * jnp.exp2(tau * column[1, :, lanes(h)])
                    a = jnp.exp2(absorb * (-0.83 * LOG2E))
                    q = (beam - passed) * inverse_of(tau)
                    ya = above * a
                    den = (1.0 + b) - ya * b
                    ti = a * inverse_of(den)
                    qb = q * b
                    th = ti * (diffuse + above * qb)
                    keep[0, l, n] = ti
                    keep[1, l, n] = b * (th + q)
                    keep[2, l, n] = 1.0 - above
                    flux[n] = (ti * (den + (ya - 1.0)), th + q * e, passed)
                for h in range(halves):
                    total[l, :, lanes(h)] += sums[h]
            return tuple(flux)

        zero = jnp.zeros((ROWS, LANES), jnp.float32)
        start = tuple(
            (zero, zero, factor[i][5] * column[0, :, lanes(h)]) for i, h in pairs
        )
        flux = lax.fori_loop(0, levels // UNROLL, down, start)
        ups = []
        for n, (i, h) in enumerate(pairs):
            above, diffuse, beam = flux[n]
            net = beam + diffuse
            ground = column[2, :, lanes(h)]
            up = ground * net / (1.0 - ground * above)
            ups.append(up)
            total[levels, :, lanes(h)] += net - (1.0 - above) * up

        def rise(step, ups):
            ups = list(ups)
            for s in range(UNROLL):
                l = levels - 1 - (step * UNROLL + s)
                sums = [None] * halves
                for n, (i, h) in enumerate(pairs):
                    ups[n] = keep[0, l, n] * ups[n] + keep[1, l, n]
                    lost = keep[2, l, n] * ups[n]
                    sums[h] = lost if sums[h] is None else sums[h] + lost
                for h in range(halves):
                    total[l, :, lanes(h)] -= sums[h]
            return tuple(ups)

        lax.fori_loop(0, levels // UNROLL, rise, tuple(ups))
        return carry

    chunks = groups * local_g // (BLOCKS * ROWS)
    set_coef(mine[...], 0)
    early = local_g // (BLOCKS * ROWS)
    lax.fori_loop(0, early, chunk, 0)
    for send in sends:
        send.wait()
    for d in range(1, groups):
        set_coef(theirs[d - 1], d * local_g)
    lax.fori_loop(early, chunks, chunk, 0)

    parts = (levels + 1) * ROWS
    flat = total[...].reshape(parts, parents)
    change = jnp.concatenate(
        [levels * (flat[: levels * ROWS] - flat[ROWS:]), flat[levels * ROWS :]], axis=0
    )
    fold_row = lax.broadcasted_iota(jnp.int32, (levels + 1, parts), 0)
    fold_lane = lax.broadcasted_iota(jnp.int32, (levels + 1, parts), 1) // ROWS
    fold = jnp.where(fold_row == fold_lane, 1.0, 0.0).astype(jnp.bfloat16)
    lit = sunlit_ref[...].astype(jnp.float32)
    rows = right_split_dot(fold, change, (((1,), (0,)), ((), ()))) * lit
    spread_out = split_dot(rows, member[...], (((1,), (0,)), ((), ())))
    heat_ref[...] = spread_out[:levels]
    surface_ref[...] = spread_out[levels:]


def body(cell_state, cell_parent, sunlit, cos_zenith, albedo, gas_optics, solar_weight):
    fields, levels, cells = cell_state.shape
    parents = sunlit.shape[0]
    local_g = gas_optics.shape[1]
    groups = lax.axis_size("ga")
    vmem = pl.BlockSpec(memory_space=pltpu.VMEM)
    count = BLOCKS * parents // LANES
    heating, surface = pl.pallas_call(
        functools.partial(kernel, groups),
        out_shape=(
            jax.ShapeDtypeStruct((levels, cells), jnp.float32),
            jax.ShapeDtypeStruct((1, cells), jnp.float32),
        ),
        in_specs=[pl.BlockSpec(memory_space=pl.ANY)] + [vmem] * 6,
        out_specs=(vmem, vmem),
        scratch_shapes=[
            pltpu.VMEM((fields, levels, cells), jnp.float32),
            pltpu.VMEM((parents, cells), jnp.bfloat16),
            pltpu.VMEM((fields, levels, ROWS, parents), jnp.float32),
            pltpu.VMEM((6, groups * local_g, LANES), jnp.float32),
            pltpu.VMEM((ROWS, LANES), jnp.float32),
            pltpu.VMEM((groups - 1, ROWS, LANES), jnp.float32),
            pltpu.VMEM((3, levels, count, ROWS, LANES), jnp.float32),
            pltpu.VMEM((levels + 1, ROWS, parents), jnp.float32),
            pltpu.VMEM((3, ROWS, parents), jnp.float32),
            pltpu.SemaphoreType.DMA((fields,)),
            pltpu.SemaphoreType.DMA((groups - 1,)),
            pltpu.SemaphoreType.DMA((groups - 1,)),
        ],
        compiler_params=pltpu.CompilerParams(
            collective_id=0, has_side_effects=True, vmem_limit_bytes=48 * 1024 * 1024
        ),
    )(
        cell_state,
        cell_parent.reshape(1, cells),
        sunlit.reshape(1, parents),
        cos_zenith.reshape(1, parents),
        albedo.reshape(1, parents),
        gas_optics,
        solar_weight.reshape(1, local_g),
    )
    return heating, surface.reshape(cells)


def solution(mesh):
    placed = (
        P(None, None, ("col", "ga")),
        P(("col", "ga")),
        P(("col", "ga")),
        P(("col", "ga")),
        P(("col", "ga")),
        P(None, "ga"),
        P("ga"),
    )
    return jax.shard_map(
        body,
        mesh=mesh,
        in_specs=placed,
        out_specs=(P(None, ("col", "ga")), P(("col", "ga"))),
        check_vma=False,
    )
```

```python
import functools

import jax
import jax.numpy as jnp
from jax import lax
from jax.experimental import pallas as pl
from jax.experimental.pallas import tpu as pltpu
from jax.sharding import PartitionSpec as P

MESH = pl.DeviceIdType.MESH
LOG2E = 1.4426950408889634
LANES = 128
ROWS = 8
BLOCKS = (3, 4, 4, 3)
GROUP = 30
RISE = 9
TERMS = 16
DEPTH = 32
FORMS = 4
NN = (((1,), (0,)), ((), ()))
NT = (((1,), (1,)), ((), ()))
TN = (((0,), (0,)), ((), ()))


def halves_of(value):
    high = value.astype(jnp.bfloat16)
    return high, (value - high.astype(jnp.float32)).astype(jnp.bfloat16)


def dot(left, right, dims):
    return lax.dot_general(left, right, dims, preferred_element_type=jnp.float32)


def kernel(
    groups,
    state_hbm,
    parent_hbm,
    sunlit_hbm,
    cosine_hbm,
    albedo_hbm,
    gas_hbm,
    weight_hbm,
    rows_ref,
    member,
    state,
    parent,
    sunlit,
    sun_angle,
    ground_row,
    gas,
    weights,
    mean,
    rhs,
    flat,
    lhs,
    solar,
    keep_even,
    keep_odd,
    beam_total,
    diffuse_total,
    lost_total,
    column,
    local_sem,
    send_sem,
    recv_sem,
):
    fields, levels, cells = state.shape
    parents = member.shape[0]
    halves = parents // LANES
    local_g = gas.shape[2]
    band = FORMS * ROWS
    starts = [sum(BLOCKS[:k]) for k in range(len(BLOCKS))]
    me = lax.axis_index("ga")

    copies = [
        pltpu.make_async_copy(source, target, local_sem.at[k])
        for k, (source, target) in enumerate(
            [
                (parent_hbm, parent),
                (gas_hbm, gas.at[0]),
                (weight_hbm, weights.at[0]),
                (state_hbm.at[0], state.at[0]),
                (state_hbm.at[1], state.at[1]),
                (state_hbm.at[2], state.at[2]),
                (cosine_hbm, sun_angle),
                (albedo_hbm, ground_row),
                (sunlit_hbm, sunlit),
            ]
        )
    ]
    for copy in copies:
        copy.start()
    barrier = pltpu.get_barrier_semaphore()
    for d in range(1, groups):
        pl.semaphore_signal(
            barrier, inc=1, device_id={"ga": lax.rem(me + d, groups)}, device_id_type=MESH
        )

    beam_total[...] = jnp.zeros_like(beam_total)
    diffuse_total[...] = jnp.zeros_like(diffuse_total)
    lost_total[...] = jnp.zeros_like(lost_total)
    rows = TERMS * (FORMS + 1)
    width = LANES * (FORMS + 1)
    row = lax.broadcasted_iota(jnp.int32, (rows, width), 0)
    lane = lax.broadcasted_iota(jnp.int32, (rows, width), 1)
    form, inner = lane // LANES, lane % LANES
    inner = jnp.where(form == 0, inner - TERMS, inner)
    pick = inner % 4 + 4 * (inner // 8)
    pick = jnp.where((form > 0) & (inner % 8 == 6), 8 + inner // 8, pick)
    hit = (form < FORMS) & (inner >= 0) & (inner < TERMS) & (row == form * TERMS + pick)
    hit = hit | ((form == FORMS) & (row >= TERMS * FORMS) & (row < TERMS * FORMS + 3))
    spread = jnp.where(hit, 1.0, 0.0).astype(jnp.bfloat16)

    def set_flat(index):
        table = gas[index]
        vapour, ozone, rayleigh, cloud = [table[k : k + 1] for k in range(4)]
        none = jnp.zeros((1, local_g), jnp.float32)
        k2 = -1.66 * LOG2E
        forms = [
            (-LOG2E * vapour, -LOG2E * ozone, -LOG2E * rayleigh, -LOG2E * cloud),
            (k2 * vapour, k2 * ozone, 0.05 * k2 * rayleigh, 0.145 * k2 * cloud),
            (none, none, 0.95 * rayleigh, 0.12825 * cloud),
            (none, none, 0.95 * rayleigh, 1.58175 * cloud),
        ]
        parts = []
        for entries in forms:
            block = jnp.concatenate(entries, axis=0)
            high = block.astype(jnp.bfloat16).astype(jnp.float32)
            low = (block - high).astype(jnp.bfloat16).astype(jnp.float32)
            rest = (block - high) - low
            parts += [high, low, rest[2:3], jnp.zeros((TERMS - 9, local_g), jnp.float32)]
        weight = weights[index]
        for k in range(3):
            high = weight.astype(jnp.bfloat16).astype(jnp.float32)
            parts.append(high)
            weight = weight - high
        parts.append(jnp.zeros((TERMS - 3, local_g), jnp.float32))
        packed = jnp.concatenate(parts, axis=0).astype(jnp.bfloat16)
        wide = dot(packed, spread, TN)
        at = pl.ds(index * local_g, local_g)
        for f in range(FORMS):
            flat[f, at, :] = wide[:, f * LANES : (f + 1) * LANES]
        solar[at, :] = wide[:, FORMS * LANES :]

    def set_lhs(k):
        for i in range(starts[k], starts[k] + BLOCKS[k]):
            at = slice(i * ROWS, (i + 1) * ROWS)
            block = jnp.concatenate([flat[f, at, :DEPTH] for f in range(FORMS)], axis=0)
            lhs[i * band : (i + 1) * band, :] = block.astype(jnp.bfloat16)

    copies[0].wait()
    local_parent = parent[...] % parents
    ids = lax.broadcasted_iota(jnp.int32, (parents, cells), 0)
    member[...] = jnp.where(ids == local_parent, 1.0, 0.0).astype(jnp.bfloat16)

    pl.semaphore_wait(barrier, groups - 1)
    sends = []
    for d in range(1, groups):
        for k, (source, target) in enumerate(((gas_hbm, gas), (weight_hbm, weights))):
            send = pltpu.make_async_remote_copy(
                src_ref=source,
                dst_ref=target.at[d],
                send_sem=send_sem.at[k, d - 1],
                recv_sem=recv_sem.at[k, d - 1],
                device_id={"ga": lax.rem(me + d, groups)},
                device_id_type=MESH,
            )
            send.start()
            sends.append(send)

    copies[1].wait()
    copies[2].wait()
    set_flat(0)
    set_lhs(0)

    for copy in copies[6:]:
        copy.wait()
    column[0] = jnp.broadcast_to(sun_angle[...], (ROWS, parents))
    column[1] = jnp.broadcast_to(1.0 / sun_angle[...], (ROWS, parents))
    column[2] = jnp.broadcast_to(ground_row[...], (ROWS, parents))
    column[3] = (-0.5 * LOG2E) * column[1]
    column[4] = (-2.0 / LOG2E) * column[0]

    for h in range(halves):
        mean[h, pl.ds(2, levels, stride=4), :] = jnp.ones((levels, LANES), jnp.float32)
    for f, r in enumerate((0, 1, 3)):
        copies[3 + f].wait()
        high, low = halves_of(state[f])
        average = 0.25 * (dot(high, member[...], NT) + dot(low, member[...], NT))
        for h in range(halves):
            mean[h, pl.ds(r, levels, stride=4), :] = average[:, h * LANES : (h + 1) * LANES]
    place = lax.broadcasted_iota(jnp.int32, (ROWS, parents), 0)
    upper = place < 4
    constant = place % 4 == 2
    for k in range(levels // 2):
        value = jnp.concatenate(
            [mean[h, k * ROWS : (k + 1) * ROWS, :] for h in range(halves)], axis=1
        )
        even, odd = [], []
        for scaled in (False, True):
            if scaled:
                value = value * column[1]
            high = value.astype(jnp.bfloat16).astype(jnp.float32)
            low = value - high
            if not scaled:
                low = jnp.where(constant, 1.0, low)
            even += [jnp.where(upper, high, pltpu.roll(low, 4, 0))] * 2
            odd += [jnp.where(upper, pltpu.roll(high, 4, 0), low)] * 2
        rhs[2 * k] = jnp.concatenate(even, axis=0).astype(jnp.bfloat16)
        rhs[2 * k + 1] = jnp.concatenate(odd, axis=0).astype(jnp.bfloat16)

    def lanes(h):
        return slice(h * LANES, (h + 1) * LANES)

    def pairs(k):
        return [(i, h) for i in range(BLOCKS[k]) for h in range(halves)]

    def optics(k, l):
        return dot(lhs[starts[k] * band : (starts[k] + BLOCKS[k]) * band], rhs[l], NN)

    def sink(k, l, flux, keep):
        forms = optics(k, l)
        flux = list(flux)
        beams = [None] * halves
        diffuses = [None] * halves
        for n, (i, h) in enumerate(pairs(k)):
            above, diffuse, beam = flux[n]
            beams[h] = beam if beams[h] is None else beams[h] + beam
            diffuses[h] = diffuse if diffuses[h] is None else diffuses[h] + diffuse
            slant, fade, b, e = [
                forms[i * band + f * ROWS : i * band + (f + 1) * ROWS, lanes(h)]
                for f in range(FORMS)
            ]
            passed = beam * jnp.exp2(slant)
            a = jnp.exp2(fade)
            q = (beam - passed) * pl.reciprocal(slant, approx=True)
            rest = above * a - 1.0
            den = 1.0 - b * rest
            ti = a * pl.reciprocal(den, approx=True)
            th = ti * (diffuse + above * (q * b))
            keep[l, 3 * n] = ti
            keep[l, 3 * n + 1] = b * (th + q)
            keep[l, 3 * n + 2] = 1.0 - above
            flux[n] = (ti * (den + rest), th + q * e, passed)
        for h in range(halves):
            beam_total[l, :, lanes(h)] += beams[h]
            diffuse_total[l, :, lanes(h)] += diffuses[h]
        return flux

    def rise(k, l, ups):
        keep = keep_even if k % 2 == 0 else keep_odd
        ups = list(ups)
        sums = [None] * halves
        for n, (i, h) in enumerate(pairs(k)):
            ups[n] = keep[l, 3 * n] * ups[n] + keep[l, 3 * n + 1]
            lost = keep[l, 3 * n + 2] * ups[n]
            sums[h] = lost if sums[h] is None else sums[h] + lost
        for h in range(halves):
            lost_total[l, :, lanes(h)] += sums[h]
        return ups

    def chunk(k, ups):
        keep = keep_even if k % 2 == 0 else keep_odd

        def down(step, carry):
            flux, ups = carry
            base = step * GROUP
            for s in range(GROUP):
                flux = sink(k, base + s, flux, keep)
                if k > 0:
                    ups = rise(k - 1, levels - 1 - base - s, ups)
            return tuple(flux), tuple(ups)

        zero = jnp.zeros((ROWS, LANES), jnp.float32)
        start = tuple(
            (
                zero,
                zero,
                solar[(starts[k] + i) * ROWS : (starts[k] + i + 1) * ROWS]
                * column[0, :, lanes(h)],
            )
            for i, h in pairs(k)
        )
        flux, unused = lax.fori_loop(0, levels // GROUP, down, (start, tuple(ups)))
        ups = []
        sums = [None] * halves
        for n, (i, h) in enumerate(pairs(k)):
            above, diffuse, beam = flux[n]
            ground, unit, scale = [column[j, :, lanes(h)] for j in (2, 3, 4)]
            up = ground * (scale * beam + diffuse) / (1.0 - ground * above)
            ups.append(up)
            net = beam + unit * (diffuse - (1.0 - above) * up)
            sums[h] = net if sums[h] is None else sums[h] + net
        for h in range(halves):
            beam_total[levels, :, lanes(h)] += sums[h]
        return tuple(ups)

    ups = chunk(0, ())
    for send in sends:
        send.wait()
    for d in range(1, groups):
        set_flat(d)
    for k in range(1, len(BLOCKS)):
        set_lhs(k)
    for k in range(1, len(BLOCKS)):
        ups = chunk(k, ups)

    def finish(step, ups):
        for s in range(RISE):
            ups = rise(len(BLOCKS) - 1, levels - 1 - step * RISE - s, ups)
        return tuple(ups)

    lax.fori_loop(0, levels // RISE, finish, ups)

    parts = (levels + 1) * ROWS
    beam_total[0:levels] += column[3] * (diffuse_total[...] - lost_total[...])
    fluxes = beam_total[...].reshape(parts, parents)
    change = jnp.concatenate(
        [levels * (fluxes[: levels * ROWS] - fluxes[ROWS:]), fluxes[levels * ROWS :]], axis=0
    )
    fold_row = lax.broadcasted_iota(jnp.int32, (levels + 1, parts), 0)
    fold_lane = lax.broadcasted_iota(jnp.int32, (levels + 1, parts), 1) // ROWS
    fold = jnp.where(fold_row == fold_lane, 1.0, 0.0).astype(jnp.bfloat16)
    high, low = halves_of(change)
    lit = sunlit[...].astype(jnp.float32)
    rows_ref[...] = (dot(fold, high, NN) + dot(fold, low, NN)) * lit


def spread_cells(rows_ref, member_ref, heat_ref, surface_ref):
    levels = heat_ref.shape[0]
    high, low = halves_of(rows_ref[...])
    cells = dot(high, member_ref[...], NN) + dot(low, member_ref[...], NN)
    heat_ref[...] = cells[:levels]
    surface_ref[...] = cells[levels:]


def body(cell_state, cell_parent, sunlit, cos_zenith, albedo, gas_optics, solar_weight):
    fields, levels, cells = cell_state.shape
    parents = sunlit.shape[0]
    local_g = gas_optics.shape[1]
    groups = lax.axis_size("ga")
    spectrum = groups * local_g
    most = max(BLOCKS)
    vmem = pl.BlockSpec(memory_space=pltpu.VMEM)
    f32 = jnp.float32
    bf16 = jnp.bfloat16
    rows, member = pl.pallas_call(
        functools.partial(kernel, groups),
        out_shape=(
            pltpu.VMEM((levels + 1, parents), f32),
            pltpu.VMEM((parents, cells), bf16),
        ),
        in_specs=[pl.BlockSpec(memory_space=pltpu.HBM)] * 7,
        out_specs=(vmem, vmem),
        scratch_shapes=[
            pltpu.VMEM((fields, levels, cells), f32),
            pltpu.VMEM((1, cells), jnp.int32),
            pltpu.VMEM((1, parents), jnp.int32),
            pltpu.VMEM((1, parents), f32),
            pltpu.VMEM((1, parents), f32),
            pltpu.VMEM((groups, 4, local_g), f32),
            pltpu.VMEM((groups, 1, local_g), f32),
            pltpu.VMEM((parents // LANES, 4 * levels, LANES), f32),
            pltpu.VMEM((levels, DEPTH, parents), bf16),
            pltpu.VMEM((FORMS, spectrum, LANES), f32),
            pltpu.VMEM((FORMS * spectrum, DEPTH), bf16),
            pltpu.VMEM((spectrum, LANES), f32),
            pltpu.VMEM((levels, 3 * most * parents // LANES, ROWS, LANES), f32),
            pltpu.VMEM((levels, 3 * most * parents // LANES, ROWS, LANES), f32),
            pltpu.VMEM((levels + 1, ROWS, parents), f32),
            pltpu.VMEM((levels, ROWS, parents), f32),
            pltpu.VMEM((levels, ROWS, parents), f32),
            pltpu.VMEM((5, ROWS, parents), f32),
            pltpu.SemaphoreType.DMA((fields + 6,)),
            pltpu.SemaphoreType.DMA((2, groups - 1)),
            pltpu.SemaphoreType.DMA((2, groups - 1)),
        ],
        compiler_params=pltpu.CompilerParams(
            collective_id=0, has_side_effects=True, vmem_limit_bytes=48 * 1024 * 1024
        ),
    )(
        *[
            pltpu.with_memory_space_constraint(value, pltpu.HBM)
            for value in (
                cell_state,
                cell_parent.reshape(1, cells),
                sunlit.reshape(1, parents),
                cos_zenith.reshape(1, parents),
                albedo.reshape(1, parents),
                gas_optics,
                solar_weight.reshape(1, local_g),
            )
        ]
    )
    heating, surface = pl.pallas_call(
        spread_cells,
        out_shape=(
            jax.ShapeDtypeStruct((levels, cells), f32),
            jax.ShapeDtypeStruct((1, cells), f32),
        ),
        in_specs=[vmem, vmem],
        out_specs=(vmem, vmem),
        compiler_params=pltpu.CompilerParams(vmem_limit_bytes=16 * 1024 * 1024),
    )(rows, member)
    return heating, surface.reshape(cells)


def solution(mesh):
    placed = (
        P(None, None, ("col", "ga")),
        P(("col", "ga")),
        P(("col", "ga")),
        P(("col", "ga")),
        P(("col", "ga")),
        P(None, "ga"),
        P("ga"),
    )
    return jax.shard_map(
        body,
        mesh=mesh,
        in_specs=placed,
        out_specs=(P(None, ("col", "ga")), P(("col", "ga"))),
        check_vma=False,
    )
```

```python
import functools

import jax
import jax.numpy as jnp
from jax import lax
from jax.experimental import pallas as pl
from jax.experimental.pallas import tpu as pltpu
from jax.sharding import PartitionSpec as P

MESH = pl.DeviceIdType.MESH
LOG2E = 1.4426950408889634
LANES = 128
ROWS = 8
BLOCKS = (3, 5, 6)
GROUP = 45
RISE = 9
TERMS = 16
DEPTH = 32
FORMS = 4
NN = (((1,), (0,)), ((), ()))
NT = (((1,), (1,)), ((), ()))
TN = (((0,), (0,)), ((), ()))


def halves_of(value):
    high = value.astype(jnp.bfloat16)
    return high, (value - high.astype(jnp.float32)).astype(jnp.bfloat16)


def dot(left, right, dims):
    return lax.dot_general(left, right, dims, preferred_element_type=jnp.float32)


def kernel(
    groups,
    state_hbm,
    parent_hbm,
    sunlit_hbm,
    cosine_hbm,
    albedo_hbm,
    gas_hbm,
    weight_hbm,
    rows_ref,
    member,
    state,
    parent,
    sunlit,
    sun_angle,
    ground_row,
    gas,
    weights,
    tables,
    parted,
    mean,
    rhs,
    flat,
    lhs,
    solar,
    keep_even,
    keep_odd,
    beam_total,
    diffuse_total,
    lost_total,
    column,
    local_sem,
    send_sem,
    recv_sem,
):
    fields, levels, cells = state.shape
    parents = member.shape[0]
    halves = parents // LANES
    local_g = gas.shape[1]
    band = FORMS * ROWS
    starts = [sum(BLOCKS[:k]) for k in range(len(BLOCKS))]
    me = lax.axis_index("ga")

    copies = [
        pltpu.make_async_copy(source, target, local_sem.at[k])
        for k, (source, target) in enumerate(
            [
                (parent_hbm, parent),
                (gas_hbm, gas),
                (weight_hbm, weights),
                (state_hbm.at[0], state.at[0]),
                (state_hbm.at[1], state.at[1]),
                (state_hbm.at[2], state.at[2]),
                (cosine_hbm, sun_angle),
                (albedo_hbm, ground_row),
                (sunlit_hbm, sunlit),
            ]
        )
    ]
    barrier = pltpu.get_barrier_semaphore()
    for d in range(1, groups):
        pl.semaphore_signal(
            barrier, inc=1, device_id={"ga": lax.rem(me + d, groups)}, device_id_type=MESH
        )
    for copy in copies:
        copy.start()

    beam_total[...] = jnp.zeros_like(beam_total)
    diffuse_total[...] = jnp.zeros_like(diffuse_total)
    lost_total[...] = jnp.zeros_like(lost_total)
    rows = TERMS * (FORMS + 1)
    width = LANES * (FORMS + 1)
    row = lax.broadcasted_iota(jnp.int32, (rows, width), 0)
    lane = lax.broadcasted_iota(jnp.int32, (rows, width), 1)
    form, inner = lane // LANES, lane % LANES
    inner = jnp.where(form == 0, inner - TERMS, inner)
    pick = inner % 4 + 4 * (inner // 8)
    pick = jnp.where((form > 0) & (inner % 8 == 6), 8 + inner // 8, pick)
    hit = (form < FORMS) & (inner >= 0) & (inner < TERMS) & (row == form * TERMS + pick)
    hit = hit | ((form == FORMS) & (row >= TERMS * FORMS) & (row < TERMS * FORMS + 3))
    spread = jnp.where(hit, 1.0, 0.0).astype(jnp.bfloat16)

    def set_flat(index):
        table = tables[index]
        vapour, ozone, rayleigh, cloud, weight = [table[k : k + 1, :local_g] for k in range(5)]
        none = jnp.zeros((1, local_g), jnp.float32)
        k2 = -1.66 * LOG2E
        forms = [
            (-LOG2E * vapour, -LOG2E * ozone, -LOG2E * rayleigh, -LOG2E * cloud),
            (k2 * vapour, k2 * ozone, 0.05 * k2 * rayleigh, 0.145 * k2 * cloud),
            (none, none, 0.95 * rayleigh, 0.12825 * cloud),
            (none, none, 0.95 * rayleigh, 1.58175 * cloud),
        ]
        parts = []
        for entries in forms:
            block = jnp.concatenate(entries, axis=0)
            high = block.astype(jnp.bfloat16).astype(jnp.float32)
            low = (block - high).astype(jnp.bfloat16).astype(jnp.float32)
            rest = (block - high) - low
            parts += [high, low, rest[2:3], jnp.zeros((TERMS - 9, local_g), jnp.float32)]
        for k in range(3):
            high = weight.astype(jnp.bfloat16).astype(jnp.float32)
            parts.append(high)
            weight = weight - high
        parts.append(jnp.zeros((TERMS - 3, local_g), jnp.float32))
        packed = jnp.concatenate(parts, axis=0).astype(jnp.bfloat16)
        wide = dot(packed, spread, TN)
        at = pl.ds(index * local_g, local_g)
        for f in range(FORMS):
            flat[f, at, :] = wide[:, f * LANES : (f + 1) * LANES]
        solar[at, :] = wide[:, FORMS * LANES :]

    def set_lhs(k):
        for i in range(starts[k], starts[k] + BLOCKS[k]):
            at = slice(i * ROWS, (i + 1) * ROWS)
            block = jnp.concatenate([flat[f, at, :DEPTH] for f in range(FORMS)], axis=0)
            lhs[i * band : (i + 1) * band, :] = block.astype(jnp.bfloat16)

    copies[1].wait()
    copies[2].wait()
    tables[0] = jnp.zeros((ROWS, LANES), jnp.float32)
    tables[0, 0:4, 0:local_g] = gas[...]
    tables[0, 4:5, 0:local_g] = weights[...]
    copies[0].wait()
    local_parent = parent[...] % parents
    ids = lax.broadcasted_iota(jnp.int32, (parents, cells), 0)
    member[...] = jnp.where(ids == local_parent, 1.0, 0.0).astype(jnp.bfloat16)

    set_flat(0)
    set_lhs(0)

    for copy in copies[6:]:
        copy.wait()
    column[0] = jnp.broadcast_to(sun_angle[...], (ROWS, parents))
    column[1] = jnp.broadcast_to(1.0 / sun_angle[...], (ROWS, parents))
    column[2] = jnp.broadcast_to(ground_row[...], (ROWS, parents))
    column[3] = (-0.5 * LOG2E) * column[1]
    column[4] = (-2.0 / LOG2E) * column[0]

    for h in range(halves):
        mean[h, pl.ds(2, levels, stride=4), :] = jnp.ones((levels, LANES), jnp.float32)
    padded = parted.shape[0] // (2 * fields)
    blank = jnp.zeros((padded - levels, cells), jnp.float32)
    for f in range(fields):
        copies[3 + f].wait()
        high, low = halves_of(jnp.concatenate([state[f], blank], axis=0))
        parted[2 * f * padded : (2 * f + 1) * padded, :] = high
        parted[(2 * f + 1) * padded : (2 * f + 2) * padded, :] = low
    sums = dot(parted[...], member[...], NT)
    for f, r in enumerate((0, 1, 3)):
        average = 0.25 * (sums[2 * f * padded :][:levels] + sums[(2 * f + 1) * padded :][:levels])
        for h in range(halves):
            mean[h, pl.ds(r, levels, stride=4), :] = average[:, h * LANES : (h + 1) * LANES]
    pl.semaphore_wait(barrier, groups - 1)
    sends = []
    for d in range(1, groups):
        send = pltpu.make_async_remote_copy(
            src_ref=tables.at[0],
            dst_ref=tables.at[d],
            send_sem=send_sem.at[d - 1],
            recv_sem=recv_sem.at[d - 1],
            device_id={"ga": lax.rem(me + d, groups)},
            device_id_type=MESH,
        )
        send.start()
        sends.append(send)

    place = lax.broadcasted_iota(jnp.int32, (ROWS, parents), 0)
    upper = place < 4
    constant = place % 4 == 2
    for k in range(levels // 2):
        value = jnp.concatenate(
            [mean[h, k * ROWS : (k + 1) * ROWS, :] for h in range(halves)], axis=1
        )
        even, odd = [], []
        for scaled in (False, True):
            if scaled:
                value = value * column[1]
            high = value.astype(jnp.bfloat16).astype(jnp.float32)
            low = value - high
            if not scaled:
                low = jnp.where(constant, 1.0, low)
            even += [jnp.where(upper, high, pltpu.roll(low, 4, 0))] * 2
            odd += [jnp.where(upper, pltpu.roll(high, 4, 0), low)] * 2
        rhs[2 * k] = jnp.concatenate(even, axis=0).astype(jnp.bfloat16)
        rhs[2 * k + 1] = jnp.concatenate(odd, axis=0).astype(jnp.bfloat16)

    def lanes(h):
        return slice(h * LANES, (h + 1) * LANES)

    def pairs(k):
        return [(i, h) for i in range(BLOCKS[k]) for h in range(halves)]

    def optics(k, l):
        return dot(lhs[starts[k] * band : (starts[k] + BLOCKS[k]) * band], rhs[l], NN)

    def sink(k, l, flux, keep):
        forms = optics(k, l)
        flux = list(flux)
        beams = [None] * halves
        diffuses = [None] * halves
        for n, (i, h) in enumerate(pairs(k)):
            above, diffuse, beam = flux[n]
            beams[h] = beam if beams[h] is None else beams[h] + beam
            diffuses[h] = diffuse if diffuses[h] is None else diffuses[h] + diffuse
            slant, fade, b, e = [
                forms[i * band + f * ROWS : i * band + (f + 1) * ROWS, lanes(h)]
                for f in range(FORMS)
            ]
            passed = beam * jnp.exp2(slant)
            a = jnp.exp2(fade)
            q = (beam - passed) * pl.reciprocal(slant, approx=True)
            rest = above * a - 1.0
            den = 1.0 - b * rest
            ti = a * pl.reciprocal(den, approx=True)
            th = ti * (diffuse + above * (q * b))
            keep[l, 3 * n] = ti
            keep[l, 3 * n + 1] = b * (th + q)
            keep[l, 3 * n + 2] = 1.0 - above
            flux[n] = (ti * (den + rest), th + q * e, passed)
        for h in range(halves):
            beam_total[l, :, lanes(h)] += beams[h]
            diffuse_total[l, :, lanes(h)] += diffuses[h]
        return flux

    def rise(k, l, ups):
        keep = keep_even if k % 2 == 0 else keep_odd
        ups = list(ups)
        sums = [None] * halves
        for n, (i, h) in enumerate(pairs(k)):
            ups[n] = keep[l, 3 * n] * ups[n] + keep[l, 3 * n + 1]
            lost = keep[l, 3 * n + 2] * ups[n]
            sums[h] = lost if sums[h] is None else sums[h] + lost
        for h in range(halves):
            lost_total[l, :, lanes(h)] += sums[h]
        return ups

    def chunk(k, ups):
        keep = keep_even if k % 2 == 0 else keep_odd

        def down(step, carry):
            flux, ups = carry
            base = step * GROUP
            for s in range(GROUP):
                flux = sink(k, base + s, flux, keep)
                if k > 0:
                    ups = rise(k - 1, levels - 1 - base - s, ups)
            return tuple(flux), tuple(ups)

        zero = jnp.zeros((ROWS, LANES), jnp.float32)
        start = tuple(
            (
                zero,
                zero,
                solar[(starts[k] + i) * ROWS : (starts[k] + i + 1) * ROWS]
                * column[0, :, lanes(h)],
            )
            for i, h in pairs(k)
        )
        flux, unused = lax.fori_loop(0, levels // GROUP, down, (start, tuple(ups)))
        ups = []
        sums = [None] * halves
        for n, (i, h) in enumerate(pairs(k)):
            above, diffuse, beam = flux[n]
            ground, unit, scale = [column[j, :, lanes(h)] for j in (2, 3, 4)]
            up = ground * (scale * beam + diffuse) / (1.0 - ground * above)
            ups.append(up)
            net = beam + unit * (diffuse - (1.0 - above) * up)
            sums[h] = net if sums[h] is None else sums[h] + net
        for h in range(halves):
            beam_total[levels, :, lanes(h)] += sums[h]
        return tuple(ups)

    ups = chunk(0, ())
    for send in sends:
        send.wait()
    for d in range(1, groups):
        set_flat(d)
    for k in range(1, len(BLOCKS)):
        set_lhs(k)
    for k in range(1, len(BLOCKS)):
        ups = chunk(k, ups)

    def finish(step, ups):
        for s in range(RISE):
            ups = rise(len(BLOCKS) - 1, levels - 1 - step * RISE - s, ups)
        return tuple(ups)

    lax.fori_loop(0, levels // RISE, finish, ups)

    parts = (levels + 1) * ROWS
    beam_total[0:levels] += column[3] * (diffuse_total[...] - lost_total[...])
    fluxes = beam_total[...].reshape(parts, parents)
    change = jnp.concatenate(
        [levels * (fluxes[: levels * ROWS] - fluxes[ROWS:]), fluxes[levels * ROWS :]], axis=0
    )
    fold_row = lax.broadcasted_iota(jnp.int32, (levels + 1, parts), 0)
    fold_lane = lax.broadcasted_iota(jnp.int32, (levels + 1, parts), 1) // ROWS
    fold = jnp.where(fold_row == fold_lane, 1.0, 0.0).astype(jnp.bfloat16)
    high, low = halves_of(change)
    lit = sunlit[...].astype(jnp.float32)
    rows_ref[...] = (dot(fold, high, NN) + dot(fold, low, NN)) * lit


def spread_cells(rows_ref, member_ref, heat_ref, surface_ref):
    levels = heat_ref.shape[0]
    high, low = halves_of(rows_ref[...])
    cells = dot(high, member_ref[...], NN) + dot(low, member_ref[...], NN)
    heat_ref[...] = cells[:levels]
    surface_ref[...] = cells[levels:]


def body(cell_state, cell_parent, sunlit, cos_zenith, albedo, gas_optics, solar_weight):
    fields, levels, cells = cell_state.shape
    parents = sunlit.shape[0]
    local_g = gas_optics.shape[1]
    groups = lax.axis_size("ga")
    spectrum = groups * local_g
    most = max(BLOCKS)
    vmem = pl.BlockSpec(memory_space=pltpu.VMEM)
    f32 = jnp.float32
    bf16 = jnp.bfloat16
    rows, member = pl.pallas_call(
        functools.partial(kernel, groups),
        out_shape=(
            pltpu.VMEM((levels + 1, parents), f32),
            pltpu.VMEM((parents, cells), bf16),
        ),
        in_specs=[pl.BlockSpec(memory_space=pltpu.HBM)] * 7,
        out_specs=(vmem, vmem),
        scratch_shapes=[
            pltpu.VMEM((fields, levels, cells), f32),
            pltpu.VMEM((1, cells), jnp.int32),
            pltpu.VMEM((1, parents), jnp.int32),
            pltpu.VMEM((1, parents), f32),
            pltpu.VMEM((1, parents), f32),
            pltpu.VMEM((4, local_g), f32),
            pltpu.VMEM((1, local_g), f32),
            pltpu.VMEM((groups, ROWS, LANES), f32),
            pltpu.VMEM((2 * fields * -(-levels // TERMS) * TERMS, cells), bf16),
            pltpu.VMEM((parents // LANES, 4 * levels, LANES), f32),
            pltpu.VMEM((levels, DEPTH, parents), bf16),
            pltpu.VMEM((FORMS, spectrum, LANES), f32),
            pltpu.VMEM((FORMS * spectrum, DEPTH), bf16),
            pltpu.VMEM((spectrum, LANES), f32),
            pltpu.VMEM((levels, 3 * most * parents // LANES, ROWS, LANES), f32),
            pltpu.VMEM((levels, 3 * most * parents // LANES, ROWS, LANES), f32),
            pltpu.VMEM((levels + 1, ROWS, parents), f32),
            pltpu.VMEM((levels, ROWS, parents), f32),
            pltpu.VMEM((levels, ROWS, parents), f32),
            pltpu.VMEM((5, ROWS, parents), f32),
            pltpu.SemaphoreType.DMA((fields + 6,)),
            pltpu.SemaphoreType.DMA((groups - 1,)),
            pltpu.SemaphoreType.DMA((groups - 1,)),
        ],
        compiler_params=pltpu.CompilerParams(
            collective_id=0, has_side_effects=True, vmem_limit_bytes=48 * 1024 * 1024
        ),
    )(
        *[
            pltpu.with_memory_space_constraint(value, pltpu.HBM)
            for value in (
                cell_state,
                cell_parent.reshape(1, cells),
                sunlit.reshape(1, parents),
                cos_zenith.reshape(1, parents),
                albedo.reshape(1, parents),
                gas_optics,
                solar_weight.reshape(1, local_g),
            )
        ]
    )
    heating, surface = pl.pallas_call(
        spread_cells,
        out_shape=(
            jax.ShapeDtypeStruct((levels, cells), f32),
            jax.ShapeDtypeStruct((1, cells), f32),
        ),
        in_specs=[vmem, vmem],
        out_specs=(vmem, vmem),
        compiler_params=pltpu.CompilerParams(vmem_limit_bytes=16 * 1024 * 1024),
    )(rows, member)
    return heating, surface.reshape(cells)


def solution(mesh):
    placed = (
        P(None, None, ("col", "ga")),
        P(("col", "ga")),
        P(("col", "ga")),
        P(("col", "ga")),
        P(("col", "ga")),
        P(None, "ga"),
        P("ga"),
    )
    return jax.shard_map(
        body,
        mesh=mesh,
        in_specs=placed,
        out_specs=(P(None, ("col", "ga")), P(("col", "ga"))),
        check_vma=False,
    )
```

```python
import functools

import jax
import jax.numpy as jnp
from jax import lax
from jax.experimental import pallas as pl
from jax.experimental.pallas import tpu as pltpu
from jax.sharding import PartitionSpec as P

MESH = pl.DeviceIdType.MESH
LOG2E = 1.4426950408889634
LANES = 128
ROWS = 8
BLOCKS = (3, 5, 6)
GROUP = 45
RISE = 9
TERMS = 16
DEPTH = 32
FORMS = 4
NN = (((1,), (0,)), ((), ()))
NT = (((1,), (1,)), ((), ()))
TN = (((0,), (0,)), ((), ()))


def halves_of(value):
    high = value.astype(jnp.bfloat16)
    return high, (value - high.astype(jnp.float32)).astype(jnp.bfloat16)


def dot(left, right, dims):
    return lax.dot_general(left, right, dims, preferred_element_type=jnp.float32)


def kernel(
    groups,
    state_hbm,
    parent_hbm,
    sunlit_hbm,
    cosine_hbm,
    albedo_hbm,
    gas_hbm,
    weight_hbm,
    rows_ref,
    member,
    state,
    parent,
    sunlit,
    sun_angle,
    ground_row,
    gas,
    weights,
    tables,
    parted,
    mean,
    rhs,
    flat,
    lhs,
    solar,
    keep_even,
    keep_odd,
    beam_total,
    diffuse_total,
    lost_total,
    column,
    local_sem,
    send_sem,
    recv_sem,
):
    fields, levels, cells = state.shape
    parents = member.shape[0]
    halves = parents // LANES
    local_g = gas.shape[1]
    band = FORMS * ROWS
    starts = [sum(BLOCKS[:k]) for k in range(len(BLOCKS))]
    me = lax.axis_index("ga")

    copies = [
        pltpu.make_async_copy(source, target, local_sem.at[k])
        for k, (source, target) in enumerate(
            [
                (parent_hbm, parent),
                (gas_hbm, gas),
                (weight_hbm, weights),
                (cosine_hbm, sun_angle),
                (albedo_hbm, ground_row),
                (sunlit_hbm, sunlit),
                (state_hbm.at[0], state.at[0]),
                (state_hbm.at[1], state.at[1]),
                (state_hbm.at[2], state.at[2]),
            ]
        )
    ]
    barrier = pltpu.get_barrier_semaphore()
    for d in range(1, groups):
        pl.semaphore_signal(
            barrier, inc=1, device_id={"ga": lax.rem(me + d, groups)}, device_id_type=MESH
        )
    for copy in copies:
        copy.start()

    beam_total[...] = jnp.zeros_like(beam_total)
    diffuse_total[...] = jnp.zeros_like(diffuse_total)
    lost_total[...] = jnp.zeros_like(lost_total)
    rows = TERMS * (FORMS + 1)
    width = LANES * (FORMS + 1)
    row = lax.broadcasted_iota(jnp.int32, (rows, width), 0)
    lane = lax.broadcasted_iota(jnp.int32, (rows, width), 1)
    form, inner = lane // LANES, lane % LANES
    inner = jnp.where(form == 0, inner - TERMS, inner)
    pick = inner % 4 + 4 * (inner // 8)
    pick = jnp.where((form > 0) & (inner % 8 == 6), 8 + inner // 8, pick)
    hit = (form < FORMS) & (inner >= 0) & (inner < TERMS) & (row == form * TERMS + pick)
    hit = hit | ((form == FORMS) & (row >= TERMS * FORMS) & (row < TERMS * FORMS + 3))
    spread = jnp.where(hit, 1.0, 0.0).astype(jnp.bfloat16)

    def set_flat(index):
        table = tables[index]
        vapour, ozone, rayleigh, cloud, weight = [table[k : k + 1, :local_g] for k in range(5)]
        none = jnp.zeros((1, local_g), jnp.float32)
        k2 = -1.66 * LOG2E
        forms = [
            (-LOG2E * vapour, -LOG2E * ozone, -LOG2E * rayleigh, -LOG2E * cloud),
            (k2 * vapour, k2 * ozone, 0.05 * k2 * rayleigh, 0.145 * k2 * cloud),
            (none, none, 0.95 * rayleigh, 0.12825 * cloud),
            (none, none, 0.95 * rayleigh, 1.58175 * cloud),
        ]
        parts = []
        for entries in forms:
            block = jnp.concatenate(entries, axis=0)
            high = block.astype(jnp.bfloat16).astype(jnp.float32)
            low = (block - high).astype(jnp.bfloat16).astype(jnp.float32)
            rest = (block - high) - low
            parts += [high, low, rest[2:3], jnp.zeros((TERMS - 9, local_g), jnp.float32)]
        for k in range(3):
            high = weight.astype(jnp.bfloat16).astype(jnp.float32)
            parts.append(high)
            weight = weight - high
        parts.append(jnp.zeros((TERMS - 3, local_g), jnp.float32))
        packed = jnp.concatenate(parts, axis=0).astype(jnp.bfloat16)
        wide = dot(packed, spread, TN)
        at = pl.ds(index * local_g, local_g)
        for f in range(FORMS):
            flat[f, at, :] = wide[:, f * LANES : (f + 1) * LANES]
        solar[at, :] = wide[:, FORMS * LANES :]

    def set_lhs(k):
        for i in range(starts[k], starts[k] + BLOCKS[k]):
            at = slice(i * ROWS, (i + 1) * ROWS)
            block = jnp.concatenate([flat[f, at, :DEPTH] for f in range(FORMS)], axis=0)
            lhs[i * band : (i + 1) * band, :] = block.astype(jnp.bfloat16)

    copies[1].wait()
    copies[2].wait()
    tables[0] = jnp.zeros((ROWS, LANES), jnp.float32)
    tables[0, 0:4, 0:local_g] = gas[...]
    tables[0, 4:5, 0:local_g] = weights[...]
    copies[0].wait()
    local_parent = parent[...] % parents
    ids = lax.broadcasted_iota(jnp.int32, (parents, cells), 0)
    member[...] = jnp.where(ids == local_parent, 1.0, 0.0).astype(jnp.bfloat16)

    set_flat(0)
    set_lhs(0)

    for copy in copies[3:6]:
        copy.wait()
    column[0] = jnp.broadcast_to(sun_angle[...], (ROWS, parents))
    column[1] = jnp.broadcast_to(1.0 / sun_angle[...], (ROWS, parents))
    column[2] = jnp.broadcast_to(ground_row[...], (ROWS, parents))
    column[3] = (-0.5 * LOG2E) * column[1]
    column[4] = (-2.0 / LOG2E) * column[0]

    for h in range(halves):
        mean[h, pl.ds(2, levels, stride=4), :] = jnp.ones((levels, LANES), jnp.float32)
    padded = parted.shape[0] // (2 * fields)
    blank = jnp.zeros((padded - levels, cells), jnp.float32)
    for f in range(fields):
        copies[6 + f].wait()
        high, low = halves_of(jnp.concatenate([state[f], blank], axis=0))
        parted[2 * f * padded : (2 * f + 1) * padded, :] = high
        parted[(2 * f + 1) * padded : (2 * f + 2) * padded, :] = low
    pl.semaphore_wait(barrier, groups - 1)
    sends = []
    for d in range(1, groups):
        send = pltpu.make_async_remote_copy(
            src_ref=tables.at[0],
            dst_ref=tables.at[d],
            send_sem=send_sem.at[d - 1],
            recv_sem=recv_sem.at[d - 1],
            device_id={"ga": lax.rem(me + d, groups)},
            device_id_type=MESH,
        )
        send.start()
        sends.append(send)

    sums = dot(parted[...], member[...], NT)
    for f, r in enumerate((0, 1, 3)):
        average = 0.25 * (sums[2 * f * padded :][:levels] + sums[(2 * f + 1) * padded :][:levels])
        for h in range(halves):
            mean[h, pl.ds(r, levels, stride=4), :] = average[:, h * LANES : (h + 1) * LANES]
    place = lax.broadcasted_iota(jnp.int32, (ROWS, parents), 0)
    upper = place < 4
    constant = place % 4 == 2
    for k in range(levels // 2):
        value = jnp.concatenate(
            [mean[h, k * ROWS : (k + 1) * ROWS, :] for h in range(halves)], axis=1
        )
        even, odd = [], []
        for scaled in (False, True):
            if scaled:
                value = value * column[1]
            high = value.astype(jnp.bfloat16).astype(jnp.float32)
            low = value - high
            if not scaled:
                low = jnp.where(constant, 1.0, low)
            even += [jnp.where(upper, high, pltpu.roll(low, 4, 0))] * 2
            odd += [jnp.where(upper, pltpu.roll(high, 4, 0), low)] * 2
        rhs[2 * k] = jnp.concatenate(even, axis=0).astype(jnp.bfloat16)
        rhs[2 * k + 1] = jnp.concatenate(odd, axis=0).astype(jnp.bfloat16)

    def lanes(h):
        return slice(h * LANES, (h + 1) * LANES)

    def pairs(k):
        return [(i, h) for i in range(BLOCKS[k]) for h in range(halves)]

    def optics(k, l):
        return dot(lhs[starts[k] * band : (starts[k] + BLOCKS[k]) * band], rhs[l], NN)

    def sink(k, l, flux, keep):
        forms = optics(k, l)
        flux = list(flux)
        beams = [None] * halves
        diffuses = [None] * halves
        for n, (i, h) in enumerate(pairs(k)):
            above, diffuse, beam = flux[n]
            beams[h] = beam if beams[h] is None else beams[h] + beam
            diffuses[h] = diffuse if diffuses[h] is None else diffuses[h] + diffuse
            slant, fade, b, e = [
                forms[i * band + f * ROWS : i * band + (f + 1) * ROWS, lanes(h)]
                for f in range(FORMS)
            ]
            passed = beam * jnp.exp2(slant)
            a = jnp.exp2(fade)
            q = (beam - passed) * pl.reciprocal(slant, approx=True)
            rest = above * a - 1.0
            den = 1.0 - b * rest
            ti = a * pl.reciprocal(den, approx=True)
            th = ti * (diffuse + above * (q * b))
            keep[l, 3 * n] = ti
            keep[l, 3 * n + 1] = b * (th + q)
            keep[l, 3 * n + 2] = 1.0 - above
            flux[n] = (ti * (den + rest), th + q * e, passed)
        for h in range(halves):
            beam_total[l, :, lanes(h)] += beams[h]
            diffuse_total[l, :, lanes(h)] += diffuses[h]
        return flux

    def rise(k, l, ups):
        keep = keep_even if k % 2 == 0 else keep_odd
        ups = list(ups)
        sums = [None] * halves
        for n, (i, h) in enumerate(pairs(k)):
            ups[n] = keep[l, 3 * n] * ups[n] + keep[l, 3 * n + 1]
            lost = keep[l, 3 * n + 2] * ups[n]
            sums[h] = lost if sums[h] is None else sums[h] + lost
        for h in range(halves):
            lost_total[l, :, lanes(h)] += sums[h]
        return ups

    def chunk(k, ups):
        keep = keep_even if k % 2 == 0 else keep_odd

        def down(step, carry):
            flux, ups = carry
            base = step * GROUP
            for s in range(GROUP):
                flux = sink(k, base + s, flux, keep)
                if k > 0:
                    ups = rise(k - 1, levels - 1 - base - s, ups)
            return tuple(flux), tuple(ups)

        zero = jnp.zeros((ROWS, LANES), jnp.float32)
        start = tuple(
            (
                zero,
                zero,
                solar[(starts[k] + i) * ROWS : (starts[k] + i + 1) * ROWS]
                * column[0, :, lanes(h)],
            )
            for i, h in pairs(k)
        )
        flux, unused = lax.fori_loop(0, levels // GROUP, down, (start, tuple(ups)))
        ups = []
        sums = [None] * halves
        for n, (i, h) in enumerate(pairs(k)):
            above, diffuse, beam = flux[n]
            ground, unit, scale = [column[j, :, lanes(h)] for j in (2, 3, 4)]
            up = ground * (scale * beam + diffuse) / (1.0 - ground * above)
            ups.append(up)
            net = beam + unit * (diffuse - (1.0 - above) * up)
            sums[h] = net if sums[h] is None else sums[h] + net
        for h in range(halves):
            beam_total[levels, :, lanes(h)] += sums[h]
        return tuple(ups)

    ups = chunk(0, ())
    for send in sends:
        send.wait()
    for d in range(1, groups):
        set_flat(d)
    for k in range(1, len(BLOCKS)):
        set_lhs(k)
    for k in range(1, len(BLOCKS)):
        ups = chunk(k, ups)

    def finish(step, ups):
        for s in range(RISE):
            ups = rise(len(BLOCKS) - 1, levels - 1 - step * RISE - s, ups)
        return tuple(ups)

    lax.fori_loop(0, levels // RISE, finish, ups)

    parts = (levels + 1) * ROWS
    beam_total[0:levels] += column[3] * (diffuse_total[...] - lost_total[...])
    fluxes = beam_total[...].reshape(parts, parents)
    change = jnp.concatenate(
        [levels * (fluxes[: levels * ROWS] - fluxes[ROWS:]), fluxes[levels * ROWS :]], axis=0
    )
    fold_row = lax.broadcasted_iota(jnp.int32, (levels + 1, parts), 0)
    fold_lane = lax.broadcasted_iota(jnp.int32, (levels + 1, parts), 1) // ROWS
    fold = jnp.where(fold_row == fold_lane, 1.0, 0.0).astype(jnp.bfloat16)
    high, low = halves_of(change)
    lit = sunlit[...].astype(jnp.float32)
    rows_ref[...] = (dot(fold, high, NN) + dot(fold, low, NN)) * lit


def spread_cells(rows_ref, member_ref, heat_ref, surface_ref):
    levels = heat_ref.shape[0]
    count = rows_ref.shape[0]
    padded = -(-count // TERMS) * TERMS
    blank = jnp.zeros((padded - count, rows_ref.shape[1]), jnp.float32)
    value = jnp.concatenate([rows_ref[...], blank], axis=0)
    both = jnp.concatenate(halves_of(value), axis=0)
    cells = dot(both, member_ref[...], NN)
    cells = cells[:padded] + cells[padded:]
    heat_ref[...] = cells[:levels]
    surface_ref[...] = cells[levels:count]


def body(cell_state, cell_parent, sunlit, cos_zenith, albedo, gas_optics, solar_weight):
    fields, levels, cells = cell_state.shape
    parents = sunlit.shape[0]
    local_g = gas_optics.shape[1]
    groups = lax.axis_size("ga")
    spectrum = groups * local_g
    most = max(BLOCKS)
    vmem = pl.BlockSpec(memory_space=pltpu.VMEM)
    f32 = jnp.float32
    bf16 = jnp.bfloat16
    rows, member = pl.pallas_call(
        functools.partial(kernel, groups),
        out_shape=(
            pltpu.VMEM((levels + 1, parents), f32),
            pltpu.VMEM((parents, cells), bf16),
        ),
        in_specs=[pl.BlockSpec(memory_space=pltpu.HBM)] * 7,
        out_specs=(vmem, vmem),
        scratch_shapes=[
            pltpu.VMEM((fields, levels, cells), f32),
            pltpu.VMEM((1, cells), jnp.int32),
            pltpu.VMEM((1, parents), jnp.int32),
            pltpu.VMEM((1, parents), f32),
            pltpu.VMEM((1, parents), f32),
            pltpu.VMEM((4, local_g), f32),
            pltpu.VMEM((1, local_g), f32),
            pltpu.VMEM((groups, ROWS, LANES), f32),
            pltpu.VMEM((2 * fields * -(-levels // TERMS) * TERMS, cells), bf16),
            pltpu.VMEM((parents // LANES, 4 * levels, LANES), f32),
            pltpu.VMEM((levels, DEPTH, parents), bf16),
            pltpu.VMEM((FORMS, spectrum, LANES), f32),
            pltpu.VMEM((FORMS * spectrum, DEPTH), bf16),
            pltpu.VMEM((spectrum, LANES), f32),
            pltpu.VMEM((levels, 3 * most * parents // LANES, ROWS, LANES), f32),
            pltpu.VMEM((levels, 3 * most * parents // LANES, ROWS, LANES), f32),
            pltpu.VMEM((levels + 1, ROWS, parents), f32),
            pltpu.VMEM((levels, ROWS, parents), f32),
            pltpu.VMEM((levels, ROWS, parents), f32),
            pltpu.VMEM((5, ROWS, parents), f32),
            pltpu.SemaphoreType.DMA((fields + 6,)),
            pltpu.SemaphoreType.DMA((groups - 1,)),
            pltpu.SemaphoreType.DMA((groups - 1,)),
        ],
        compiler_params=pltpu.CompilerParams(
            collective_id=0, has_side_effects=True, vmem_limit_bytes=48 * 1024 * 1024
        ),
    )(
        *[
            pltpu.with_memory_space_constraint(value, pltpu.HBM)
            for value in (
                cell_state,
                cell_parent.reshape(1, cells),
                sunlit.reshape(1, parents),
                cos_zenith.reshape(1, parents),
                albedo.reshape(1, parents),
                gas_optics,
                solar_weight.reshape(1, local_g),
            )
        ]
    )
    heating, surface = pl.pallas_call(
        spread_cells,
        out_shape=(
            jax.ShapeDtypeStruct((levels, cells), f32),
            jax.ShapeDtypeStruct((1, cells), f32),
        ),
        in_specs=[vmem, vmem],
        out_specs=(vmem, vmem),
        compiler_params=pltpu.CompilerParams(vmem_limit_bytes=16 * 1024 * 1024),
    )(rows, member)
    return heating, surface.reshape(cells)


def solution(mesh):
    placed = (
        P(None, None, ("col", "ga")),
        P(("col", "ga")),
        P(("col", "ga")),
        P(("col", "ga")),
        P(("col", "ga")),
        P(None, "ga"),
        P("ga"),
    )
    return jax.shard_map(
        body,
        mesh=mesh,
        in_specs=placed,
        out_specs=(P(None, ("col", "ga")), P(("col", "ga"))),
        check_vma=False,
    )
```

```python
import functools

import jax
import jax.numpy as jnp
from jax import lax
from jax.experimental import pallas as pl
from jax.experimental.pallas import tpu as pltpu
from jax.sharding import PartitionSpec as P

MESH = pl.DeviceIdType.MESH
LOG2E = 1.4426950408889634
LANES = 128
ROWS = 8
BLOCKS = (3, 5, 6)
GROUP = 45
RISE = 9
TERMS = 16
DEPTH = 32
FORMS = 4
NN = (((1,), (0,)), ((), ()))
NT = (((1,), (1,)), ((), ()))
TN = (((0,), (0,)), ((), ()))


def halves_of(value):
    high = value.astype(jnp.bfloat16)
    return high, (value - high.astype(jnp.float32)).astype(jnp.bfloat16)


def dot(left, right, dims):
    return lax.dot_general(left, right, dims, preferred_element_type=jnp.float32)


def kernel(
    groups,
    state_hbm,
    parent_hbm,
    sunlit_hbm,
    cosine_hbm,
    albedo_hbm,
    gas_hbm,
    weight_hbm,
    rows_ref,
    member,
    state,
    parent,
    sunlit,
    sun_angle,
    ground_row,
    gas,
    weights,
    tables,
    parted,
    mean,
    rhs,
    flat,
    lhs,
    solar,
    keep_even,
    keep_odd,
    beam_total,
    diffuse_total,
    lost_total,
    column,
    local_sem,
    send_sem,
    recv_sem,
):
    fields, levels, cells = state.shape
    parents = member.shape[0]
    halves = parents // LANES
    local_g = gas.shape[1]
    band = FORMS * ROWS
    starts = [sum(BLOCKS[:k]) for k in range(len(BLOCKS))]
    me = lax.axis_index("ga")

    copies = [
        pltpu.make_async_copy(source, target, local_sem.at[k])
        for k, (source, target) in enumerate(
            [
                (parent_hbm, parent),
                (gas_hbm, gas),
                (weight_hbm, weights),
                (cosine_hbm, sun_angle),
                (albedo_hbm, ground_row),
                (sunlit_hbm, sunlit),
                (state_hbm.at[0], state.at[0]),
                (state_hbm.at[1], state.at[1]),
                (state_hbm.at[2], state.at[2]),
            ]
        )
    ]
    barrier = pltpu.get_barrier_semaphore()
    for d in range(1, groups):
        pl.semaphore_signal(
            barrier, inc=1, device_id={"ga": lax.rem(me + d, groups)}, device_id_type=MESH
        )
    for copy in copies:
        copy.start()

    beam_total[...] = jnp.zeros_like(beam_total)
    diffuse_total[...] = jnp.zeros_like(diffuse_total)
    lost_total[...] = jnp.zeros_like(lost_total)
    rows = TERMS * (FORMS + 1)
    width = LANES * (FORMS + 1)
    row = lax.broadcasted_iota(jnp.int32, (rows, width), 0)
    lane = lax.broadcasted_iota(jnp.int32, (rows, width), 1)
    form, inner = lane // LANES, lane % LANES
    inner = jnp.where(form == 0, inner - TERMS, inner)
    pick = inner % 4 + 4 * (inner // 8)
    pick = jnp.where((form > 0) & (inner % 8 == 6), 8 + inner // 8, pick)
    hit = (form < FORMS) & (inner >= 0) & (inner < TERMS) & (row == form * TERMS + pick)
    hit = hit | ((form == FORMS) & (row >= TERMS * FORMS) & (row < TERMS * FORMS + 3))
    spread = jnp.where(hit, 1.0, 0.0).astype(jnp.bfloat16)

    def set_flat(index):
        table = tables[index]
        vapour, ozone, rayleigh, cloud, weight = [table[k : k + 1, :local_g] for k in range(5)]
        none = jnp.zeros((1, local_g), jnp.float32)
        k2 = -1.66 * LOG2E
        forms = [
            (-LOG2E * vapour, -LOG2E * ozone, -LOG2E * rayleigh, -LOG2E * cloud),
            (k2 * vapour, k2 * ozone, 0.05 * k2 * rayleigh, 0.145 * k2 * cloud),
            (none, none, 0.95 * rayleigh, 0.12825 * cloud),
            (none, none, 0.95 * rayleigh, 1.58175 * cloud),
        ]
        parts = []
        for entries in forms:
            block = jnp.concatenate(entries, axis=0)
            high = block.astype(jnp.bfloat16).astype(jnp.float32)
            low = (block - high).astype(jnp.bfloat16).astype(jnp.float32)
            rest = (block - high) - low
            parts += [high, low, rest[2:3], jnp.zeros((TERMS - 9, local_g), jnp.float32)]
        for k in range(3):
            high = weight.astype(jnp.bfloat16).astype(jnp.float32)
            parts.append(high)
            weight = weight - high
        parts.append(jnp.zeros((TERMS - 3, local_g), jnp.float32))
        packed = jnp.concatenate(parts, axis=0).astype(jnp.bfloat16)
        wide = dot(packed, spread, TN)
        at = pl.ds(index * local_g, local_g)
        for f in range(FORMS):
            flat[f, at, :] = wide[:, f * LANES : (f + 1) * LANES]
        solar[at, :] = wide[:, FORMS * LANES :]

    def set_lhs(k):
        for i in range(starts[k], starts[k] + BLOCKS[k]):
            at = slice(i * ROWS, (i + 1) * ROWS)
            block = jnp.concatenate([flat[f, at, :DEPTH] for f in range(FORMS)], axis=0)
            lhs[i * band : (i + 1) * band, :] = block.astype(jnp.bfloat16)

    copies[1].wait()
    copies[2].wait()
    tables[0] = jnp.zeros((ROWS, LANES), jnp.float32)
    tables[0, 0:4, 0:local_g] = gas[...]
    tables[0, 4:5, 0:local_g] = weights[...]
    copies[0].wait()
    local_parent = parent[...] % parents
    ids = lax.broadcasted_iota(jnp.int32, (parents, cells), 0)
    member[...] = jnp.where(ids == local_parent, 1.0, 0.0).astype(jnp.bfloat16)

    set_flat(0)
    set_lhs(0)

    for copy in copies[3:6]:
        copy.wait()
    column[0] = jnp.broadcast_to(sun_angle[...], (ROWS, parents))
    column[1] = jnp.broadcast_to(1.0 / sun_angle[...], (ROWS, parents))
    column[2] = jnp.broadcast_to(ground_row[...], (ROWS, parents))
    column[3] = (-0.5 * LOG2E) * column[1]
    column[4] = (-2.0 / LOG2E) * column[0]

    for h in range(halves):
        mean[h, pl.ds(2, levels, stride=4), :] = jnp.ones((levels, LANES), jnp.float32)
    padded = parted.shape[0] // (2 * fields)
    blank = jnp.zeros((padded - levels, cells), jnp.float32)
    for f in range(fields):
        copies[6 + f].wait()
        high, low = halves_of(jnp.concatenate([state[f], blank], axis=0))
        parted[2 * f * padded : (2 * f + 1) * padded, :] = high
        parted[(2 * f + 1) * padded : (2 * f + 2) * padded, :] = low
    pl.semaphore_wait(barrier, groups - 1)
    sends = []
    for d in range(1, groups):
        send = pltpu.make_async_remote_copy(
            src_ref=tables.at[0],
            dst_ref=tables.at[d],
            send_sem=send_sem.at[d - 1],
            recv_sem=recv_sem.at[d - 1],
            device_id={"ga": lax.rem(me + d, groups)},
            device_id_type=MESH,
        )
        send.start()
        sends.append(send)

    sums = dot(parted[...], member[...], NT)
    for f, r in enumerate((0, 1, 3)):
        average = 0.25 * (sums[2 * f * padded :][:levels] + sums[(2 * f + 1) * padded :][:levels])
        for h in range(halves):
            mean[h, pl.ds(r, levels, stride=4), :] = average[:, h * LANES : (h + 1) * LANES]
    place = lax.broadcasted_iota(jnp.int32, (ROWS, parents), 0)
    upper = place < 4
    constant = place % 4 == 2
    for k in range(levels // 2):
        value = jnp.concatenate(
            [mean[h, k * ROWS : (k + 1) * ROWS, :] for h in range(halves)], axis=1
        )
        even, odd = [], []
        for scaled in (False, True):
            if scaled:
                value = value * column[1]
            high = value.astype(jnp.bfloat16).astype(jnp.float32)
            low = value - high
            if not scaled:
                low = jnp.where(constant, 1.0, low)
            even += [jnp.where(upper, high, pltpu.roll(low, 4, 0))] * 2
            odd += [jnp.where(upper, pltpu.roll(high, 4, 0), low)] * 2
        rhs[2 * k] = jnp.concatenate(even, axis=0).astype(jnp.bfloat16)
        rhs[2 * k + 1] = jnp.concatenate(odd, axis=0).astype(jnp.bfloat16)

    def lanes(h):
        return slice(h * LANES, (h + 1) * LANES)

    def pairs(k):
        return [(i, h) for i in range(BLOCKS[k]) for h in range(halves)]

    def optics(k, l):
        return dot(lhs[starts[k] * band : (starts[k] + BLOCKS[k]) * band], rhs[l], NN)

    def sink(k, l, flux, keep):
        forms = optics(k, l)
        flux = list(flux)
        beams = [None] * halves
        diffuses = [None] * halves
        for n, (i, h) in enumerate(pairs(k)):
            above, diffuse, beam = flux[n]
            beams[h] = beam if beams[h] is None else beams[h] + beam
            diffuses[h] = diffuse if diffuses[h] is None else diffuses[h] + diffuse
            slant, fade, b, e = [
                forms[i * band + f * ROWS : i * band + (f + 1) * ROWS, lanes(h)]
                for f in range(FORMS)
            ]
            passed = beam * jnp.exp2(slant)
            a = jnp.exp2(fade)
            q = (beam - passed) * pl.reciprocal(slant, approx=True)
            rest = above * a - 1.0
            den = 1.0 - b * rest
            ti = a * pl.reciprocal(den, approx=True)
            th = ti * (diffuse + above * (q * b))
            keep[l, 3 * n] = ti
            keep[l, 3 * n + 1] = b * (th + q)
            keep[l, 3 * n + 2] = 1.0 - above
            flux[n] = (ti * (den + rest), th + q * e, passed)
        for h in range(halves):
            beam_total[l, :, lanes(h)] += beams[h]
            diffuse_total[l, :, lanes(h)] += diffuses[h]
        return flux

    def rise(k, l, ups):
        keep = keep_even if k % 2 == 0 else keep_odd
        ups = list(ups)
        sums = [None] * halves
        for n, (i, h) in enumerate(pairs(k)):
            ups[n] = keep[l, 3 * n] * ups[n] + keep[l, 3 * n + 1]
            lost = keep[l, 3 * n + 2] * ups[n]
            sums[h] = lost if sums[h] is None else sums[h] + lost
        for h in range(halves):
            lost_total[l, :, lanes(h)] += sums[h]
        return ups

    def chunk(k, ups):
        keep = keep_even if k % 2 == 0 else keep_odd

        def down(step, carry):
            flux, ups = carry
            base = step * GROUP
            for s in range(GROUP):
                flux = sink(k, base + s, flux, keep)
                if k > 0:
                    ups = rise(k - 1, levels - 1 - base - s, ups)
            return tuple(flux), tuple(ups)

        zero = jnp.zeros((ROWS, LANES), jnp.float32)
        start = tuple(
            (
                zero,
                zero,
                solar[(starts[k] + i) * ROWS : (starts[k] + i + 1) * ROWS]
                * column[0, :, lanes(h)],
            )
            for i, h in pairs(k)
        )
        flux, unused = lax.fori_loop(0, levels // GROUP, down, (start, tuple(ups)))
        ups = []
        sums = [None] * halves
        for n, (i, h) in enumerate(pairs(k)):
            above, diffuse, beam = flux[n]
            ground, unit, scale = [column[j, :, lanes(h)] for j in (2, 3, 4)]
            up = ground * (scale * beam + diffuse) / (1.0 - ground * above)
            ups.append(up)
            net = beam + unit * (diffuse - (1.0 - above) * up)
            sums[h] = net if sums[h] is None else sums[h] + net
        for h in range(halves):
            beam_total[levels, :, lanes(h)] += sums[h]
        return tuple(ups)

    ups = chunk(0, ())
    for send in sends:
        send.wait()
    for d in range(1, groups):
        set_flat(d)
    for k in range(1, len(BLOCKS)):
        set_lhs(k)
    for k in range(1, len(BLOCKS)):
        ups = chunk(k, ups)

    def finish(step, ups):
        for s in range(RISE):
            ups = rise(len(BLOCKS) - 1, levels - 1 - step * RISE - s, ups)
        return tuple(ups)

    lax.fori_loop(0, levels // RISE, finish, ups)

    parts = (levels + 1) * ROWS
    beam_total[0:levels] += column[3] * (diffuse_total[...] - lost_total[...])
    fluxes = beam_total[...].reshape(parts, parents)
    change = jnp.concatenate(
        [levels * (fluxes[: levels * ROWS] - fluxes[ROWS:]), fluxes[levels * ROWS :]], axis=0
    )
    fold_row = lax.broadcasted_iota(jnp.int32, (levels + 1, parts), 0)
    fold_lane = lax.broadcasted_iota(jnp.int32, (levels + 1, parts), 1) // ROWS
    fold = jnp.where(fold_row == fold_lane, 1.0, 0.0).astype(jnp.bfloat16)
    high, low = halves_of(change)
    lit = sunlit[...].astype(jnp.float32)
    rows_ref[...] = (dot(fold, high, NN) + dot(fold, low, NN)) * lit


def spread_cells(rows_ref, member_ref, heat_ref, surface_ref):
    levels = heat_ref.shape[0]
    count = rows_ref.shape[0]
    padded = -(-count // TERMS) * TERMS
    blank = jnp.zeros((padded - count, rows_ref.shape[1]), jnp.float32)
    value = jnp.concatenate([rows_ref[...], blank], axis=0)
    both = jnp.concatenate(halves_of(value), axis=0)
    cells = dot(both, member_ref[...], NN)
    cells = cells[:padded] + cells[padded:]
    heat_ref[...] = cells[:levels]
    surface_ref[...] = cells[levels:count]


def body(cell_state, cell_parent, sunlit, cos_zenith, albedo, gas_optics, solar_weight):
    fields, levels, cells = cell_state.shape
    parents = sunlit.shape[0]
    local_g = gas_optics.shape[1]
    groups = lax.axis_size("ga")
    spectrum = groups * local_g
    most = max(BLOCKS)
    vmem = pl.BlockSpec(memory_space=pltpu.VMEM)
    f32 = jnp.float32
    bf16 = jnp.bfloat16
    rows, member = pl.pallas_call(
        functools.partial(kernel, groups),
        out_shape=(
            pltpu.VMEM((levels + 1, parents), f32),
            pltpu.VMEM((parents, cells), bf16),
        ),
        in_specs=[pl.BlockSpec(memory_space=pltpu.HBM)] * 7,
        out_specs=(vmem, vmem),
        scratch_shapes=[
            pltpu.VMEM((fields, levels, cells), f32),
            pltpu.VMEM((1, cells), jnp.int32),
            pltpu.VMEM((1, parents), jnp.int32),
            pltpu.VMEM((1, parents), f32),
            pltpu.VMEM((1, parents), f32),
            pltpu.VMEM((4, local_g), f32),
            pltpu.VMEM((1, local_g), f32),
            pltpu.VMEM((groups, ROWS, LANES), f32),
            pltpu.VMEM((2 * fields * -(-levels // TERMS) * TERMS, cells), bf16),
            pltpu.VMEM((parents // LANES, 4 * -(-levels // ROWS) * ROWS + ROWS, LANES), f32),
            pltpu.VMEM((levels, DEPTH, parents), bf16),
            pltpu.VMEM((FORMS, spectrum + ROWS, LANES), f32),
            pltpu.VMEM((FORMS * spectrum, DEPTH), bf16),
            pltpu.VMEM((spectrum + ROWS, LANES), f32),
            pltpu.VMEM((levels, 3 * most * parents // LANES, ROWS, LANES), f32),
            pltpu.VMEM((levels, 3 * most * parents // LANES, ROWS, LANES), f32),
            pltpu.VMEM((levels + 1, ROWS, parents), f32),
            pltpu.VMEM((levels, ROWS, parents), f32),
            pltpu.VMEM((levels, ROWS, parents), f32),
            pltpu.VMEM((5, ROWS, parents), f32),
            pltpu.SemaphoreType.DMA((fields + 6,)),
            pltpu.SemaphoreType.DMA((groups - 1,)),
            pltpu.SemaphoreType.DMA((groups - 1,)),
        ],
        compiler_params=pltpu.CompilerParams(
            collective_id=0, has_side_effects=True, vmem_limit_bytes=48 * 1024 * 1024
        ),
    )(
        *[
            pltpu.with_memory_space_constraint(value, pltpu.HBM)
            for value in (
                cell_state,
                cell_parent.reshape(1, cells),
                sunlit.reshape(1, parents),
                cos_zenith.reshape(1, parents),
                albedo.reshape(1, parents),
                gas_optics,
                solar_weight.reshape(1, local_g),
            )
        ]
    )
    heating, surface = pl.pallas_call(
        spread_cells,
        out_shape=(
            jax.ShapeDtypeStruct((levels, cells), f32),
            jax.ShapeDtypeStruct((1, cells), f32),
        ),
        in_specs=[vmem, vmem],
        out_specs=(vmem, vmem),
        compiler_params=pltpu.CompilerParams(vmem_limit_bytes=16 * 1024 * 1024),
    )(rows, member)
    return heating, surface.reshape(cells)


def solution(mesh):
    placed = (
        P(None, None, ("col", "ga")),
        P(("col", "ga")),
        P(("col", "ga")),
        P(("col", "ga")),
        P(("col", "ga")),
        P(None, "ga"),
        P("ga"),
    )
    return jax.shard_map(
        body,
        mesh=mesh,
        in_specs=placed,
        out_specs=(P(None, ("col", "ga")), P(("col", "ga"))),
        check_vma=False,
    )
```
